32 devices in a mesh: groups: 2 (over x), rows: 16 (over z, y, core).
Axes of the slice: x: 2, y: 2, z: 4, core: 2. Of those that a mesh axis runs over, the one named last changes fastest.
Arguments:
- response: float32 [1536, 128, 128], P(('groups', 'rows')), parts along dimension 0, may hold values from 0.0001 to 0.01
- block_row: int32 [1536], P(('groups', 'rows')), parts along dimension 0, may hold values from 0 to 7, as said below
- block_col: int32 [1536], P(('groups', 'rows')), parts along dimension 0, may hold values from 0 to 207, as said below
- counts: int32 [64, 32768], P(None, ('groups', 'rows')), parts along dimension 1, may hold values from 1 to 16
- prior: float32 [53248], P(('groups', 'rows')), parts along dimension 0, may hold values from 0.5 to 5
Outputs:
- unfolded: float32 [64, 53248], P(None, ('groups', 'rows')), parts along dimension 1
The draws below stay inside these ranges and needn't reach their ends.
There are 2 independent parts, one for each index of `groups`. The reference program is written for one: setup_inputs(seed, part) draws one part's arguments, and reference() takes and returns one part's arrays. A program takes and returns all parts, laid end to end along the dimension named above; each array names one. Nothing has to cross between parts.
Inputs may be any that keep to these rules, and one draw needn't show every extreme that they name: `block_col`: each device's 48 blocks come in 16 groups of 3; group o holds block columns o * 13 to (o + 1) * 13 - 1, distinct within the group; every block column holds at least one block. `block_row`: every block row of every device holds at least one block.
All inputs are finite; a program needn't handle non-finite values.
Results may differ from the reference program's by a relative error of at most 0.0001.
Values sent between devices are 32-bit elements; how exact they have to be, the bound alone decides.
A program may use at most 128 MiB of HBM per device.

```python
import math
import jax
import jax.numpy as jnp
from jax import lax

BLK = 128
REP = 64
BR_DEV = 8
BC_DEV = 13
CAP = 3
ITERS = 2
NBLK = 768
NT = 26624
NRECO = 16384
N_ROWS = 16


def draw_block_row(key, part):
    key = jax.random.fold_in(key, 11)
    pattern = (jnp.arange(N_ROWS * CAP, dtype=jnp.int32) % BR_DEV).astype(jnp.int32)
    subkeys = jax.random.split(key, N_ROWS)
    shuffled = jax.vmap(lambda subkey: jax.random.permutation(subkey, pattern))(subkeys)
    return shuffled.reshape(-1).astype(jnp.int32)


def draw_block_col(key, part):
    key = jax.random.fold_in(key, 23)
    subkeys = jax.random.split(key, N_ROWS)
    orders = jax.vmap(lambda subkey: jax.random.permutation(subkey, BC_DEV))(subkeys).astype(jnp.int32)
    device_ids = jnp.arange(N_ROWS, dtype=jnp.int32)[:, None, None]
    owner_ids = jnp.arange(N_ROWS, dtype=jnp.int32)[None, :, None]
    within = jnp.arange(CAP, dtype=jnp.int32)[None, None, :]
    position = (device_ids * CAP + within) % BC_DEV
    owner_full = jnp.broadcast_to(owner_ids, (N_ROWS, N_ROWS, CAP))
    position_full = jnp.broadcast_to(position, (N_ROWS, N_ROWS, CAP))
    local_column = orders[owner_full, position_full]
    columns = owner_full * BC_DEV + local_column
    return columns.reshape(-1).astype(jnp.int32)


def touch_ends(entries, key, low, top_value):
    place = [jax.random.randint(jax.random.fold_in(key, axis), (), 0, length) for axis, length in enumerate(entries.shape)]
    main_axis = entries.shape.index(max(entries.shape))
    neighbour = place[:main_axis] + [(place[main_axis] + 1) % entries.shape[main_axis]] + place[main_axis + 1:]
    return entries.at[tuple(place)].set(low).at[tuple(neighbour)].set(top_value)


def block_scale(key, dims, cuts, smallest, largest):
    def one(dim, parts):
        draws = jax.random.uniform(jax.random.fold_in(jax.random.fold_in(key, 6), dim), (parts,), jnp.float32, smallest / len(cuts), largest / len(cuts))
        return jnp.repeat(jnp.exp(draws), dims[dim] // parts).reshape((-1,) + (1,) * (len(dims) - dim - 1))

    gain = one(*cuts[0])
    for cut in cuts[1:]:
        gain = gain * one(*cut)
    return gain


def setup_inputs(seed: int = 0, part: int = 0) -> dict:
    streams_of = jax.random.split(jax.random.key(seed), 6)
    part_keys = jax.random.split(jax.random.fold_in(streams_of[5], part), 6)
    return {
        "response": jnp.clip(jnp.exp(math.log(0.01) - 4.6051702 * jax.random.uniform(part_keys[0], (NBLK, BLK, BLK), jnp.float32) ** block_scale(part_keys[0], (NBLK, BLK, BLK), ((0, 16),), -0.2, 0.2)), 0.0001, 0.01),
        "block_row": draw_block_row(jax.random.fold_in(jax.random.fold_in(streams_of[5], part), 71), part),
        "block_col": draw_block_col(jax.random.fold_in(jax.random.fold_in(streams_of[5], part), 71), part),
        "counts": touch_ends(jax.random.randint(part_keys[3], (REP, NRECO), 1, 17), jax.random.fold_in(part_keys[3], 1), 1, 16).astype(jnp.int32),
        "prior": jnp.clip(jnp.exp(math.log(5.0) - 2.3025851 * jax.random.uniform(part_keys[4], (NT,), jnp.float32) ** block_scale(part_keys[4], (NT,), ((0, 16),), -0.2, 0.2)), 0.5, 5.0),
    }


def reference(response, block_row, block_col, counts, prior):
    block_total = response.shape[0]
    slot_count = N_ROWS * CAP
    row_blocks = BR_DEV * N_ROWS
    col_blocks = BC_DEV * N_ROWS
    device_of = (jnp.arange(block_total, dtype=jnp.int32) // slot_count).astype(jnp.int32)
    row_global = (device_of * BR_DEV + block_row).astype(jnp.int32)
    col_global = block_col.astype(jnp.int32)
    column_mass = jnp.sum(response, axis=1)
    efficiency = jax.ops.segment_sum(column_mass, col_global, col_blocks)
    prior_blocks = prior.reshape(col_blocks, BLK)
    estimate = jnp.broadcast_to(prior_blocks[:, None, :], (col_blocks, REP, BLK))
    measured = counts.reshape(REP, row_blocks, BLK).transpose(1, 0, 2).astype(jnp.float32)
    for iteration in range(ITERS):
        fetched = estimate[col_global]
        contrib = jnp.einsum("sic,src->sri", response, fetched, precision=lax.Precision.HIGHEST)
        folded = jax.ops.segment_sum(contrib, row_global, row_blocks)
        ratios = measured / folded
        backward = jnp.einsum("sic,sri->src", response, ratios[row_global], precision=lax.Precision.HIGHEST)
        gathered = jax.ops.segment_sum(backward, col_global, col_blocks)
        estimate = estimate * gathered / efficiency[:, None, :]
    return estimate.transpose(1, 0, 2).reshape(REP, col_blocks * BLK)
```

```python
import functools

import jax
import jax.numpy as jnp
from jax import lax
from jax.experimental import pallas as pl
from jax.experimental.pallas import tpu as pltpu
from jax.sharding import PartitionSpec as P

CHUNKS = 2
F32 = jnp.float32
BF16 = jnp.bfloat16


def split(x):
    high = x.astype(BF16).astype(F32)
    return jnp.concatenate([high, x - high], axis=0).astype(BF16)


def kernel(
    n, per, cols, rows, chunk_count,
    response, block_row, local_col, col_message, counts, prior,
    out,
    response_split, message, meta, wanted_landed, wanted, send, returned, fetched, estimate,
    ratio, inverse, send_sem, recv_sem, local_sem,
):
    blk = prior.shape[1]
    rc = counts.shape[0] // chunk_count
    me = lax.axis_index("rows")

    def peer_of(k):
        return lax.rem(me + k + 1, n)

    def remote(src, dst, index, peer):
        return pltpu.make_async_remote_copy(
            src_ref=src, dst_ref=dst, send_sem=send_sem.at[index], recv_sem=recv_sem.at[index],
            device_id={"rows": peer}, device_id_type=pl.DeviceIdType.MESH,
        )

    def wait_bytes(ref, sem):
        pltpu.make_async_copy(ref, ref, sem).wait()

    barrier = pltpu.get_barrier_semaphore()

    @pl.loop(0, n - 1)
    def _(k):
        pl.semaphore_signal(
            barrier, inc=1, device_id={"rows": peer_of(k)}, device_id_type=pl.DeviceIdType.MESH
        )

    @pl.loop(0, n)
    def _(p):
        message[p, 0:cols, :] = prior[...]
        for j in range(per):
            block = response[p * per + j]
            message[p, cols + j : cols + j + 1, :] = jnp.sum(block, axis=0, keepdims=True)
            response_split[p * per + j] = split(block)

    pl.semaphore_wait(barrier, n - 1)
    meta_index = 3 * chunk_count

    @pl.loop(0, n - 1)
    def _(k):
        peer = peer_of(k)
        remote(message.at[peer], meta.at[me], meta_index, peer).start()
        remote(col_message.at[peer], wanted_landed.at[me], meta_index + 1, peer).start()

    meta[me] = message[me]
    wanted_landed[me] = col_message[me]
    wait_bytes(meta.at[pl.ds(0, n - 1)], recv_sem.at[meta_index])

    def fold_prior(p, total):
        for j in range(per):
            s = p * per + j
            row = meta[p, pl.ds(local_col[s], 1), :]
            place = lax.broadcasted_iota(jnp.int32, (rows, blk), 0) == block_row[s]
            masked = jnp.where(place, jnp.broadcast_to(row, (rows, blk)), 0.0)
            total = total + lax.dot_general(
                split(masked), response_split[s], (((1,), (1,)), ((), ())), preferred_element_type=F32
            )
        return total

    total = lax.fori_loop(0, n, fold_prior, jnp.zeros((2 * rows, 2 * blk), F32))
    total = total[:rows] + total[rows:]
    first_fold = total[:, :blk] + total[:, blk:]

    def store_ratio(c, b, folded):
        measured = counts[c * rc : (c + 1) * rc, b * blk : (b + 1) * blk].astype(F32)
        ratio[b * chunk_count + c] = split(measured / folded)

    def backward(c, phase):
        def one(s):
            x = ratio[block_row[s] * chunk_count + c]
            both = jnp.dot(
                jnp.concatenate([x, x], axis=1), response_split[s], preferred_element_type=F32
            )
            return both[:rc] + both[rc:]

        @pl.loop(0, n - 1)
        def _(k):
            peer = peer_of(k)
            for j in range(per):
                send[c, peer * per + j] = one(peer * per + j)
            remote(
                send.at[c, pl.ds(peer * per, per)], returned.at[c, pl.ds(me * per, per)],
                phase * chunk_count + c, peer,
            ).start()

        for j in range(per):
            returned[c, me * per + j] = one(me * per + j)

    def wait_sent(c, phase):
        wait_bytes(send.at[c, pl.ds(0, (n - 1) * per)], send_sem.at[phase * chunk_count + c])

    def gather(c, phase):
        wait_bytes(returned.at[c, pl.ds(0, (n - 1) * per)], recv_sem.at[phase * chunk_count + c])

        def add(p, sums):
            sums = list(sums)
            for j in range(per):
                block = returned[c, p * per + j]
                w = wanted[p, 0, j]
                for k in range(cols):
                    sums[k] = sums[k] + block * (w == k).astype(F32)
            return tuple(sums)

        return lax.fori_loop(0, n, add, tuple(jnp.zeros((rc, blk), F32) for _ in range(cols)))

    def spread(c):
        @pl.loop(0, n - 1)
        def _(k):
            peer = peer_of(k)
            for j in range(per):
                send[c, peer * per + j] = estimate[c * cols + wanted[peer, 0, j]]
            remote(
                send.at[c, pl.ds(peer * per, per)], fetched.at[c, pl.ds(me * per, per)],
                chunk_count + c, peer,
            ).start()

        for j in range(per):
            fetched[c, me * per + j] = estimate[c * cols + wanted[me, 0, j]]

    def fold(c):
        wait_bytes(fetched.at[c, pl.ds(0, (n - 1) * per)], recv_sem.at[chunk_count + c])

        def add(p, sums):
            sums = list(sums)
            for j in range(per):
                s = p * per + j
                product = lax.dot_general(
                    split(fetched[c, s]), response_split[s], (((1,), (1,)), ((), ())),
                    preferred_element_type=F32,
                )
                product = product[:rc] + product[rc:]
                product = product[:, :blk] + product[:, blk:]
                r = block_row[s]
                for b in range(rows):
                    sums[b] = sums[b] + product * (r == b).astype(F32)
            return tuple(sums)

        sums = lax.fori_loop(0, n, add, tuple(jnp.zeros((rc, blk), F32) for _ in range(rows)))
        for b in range(rows):
            store_ratio(c, b, sums[b])

    for c in range(chunk_count):
        for b in range(rows):
            store_ratio(c, b, first_fold[b : b + 1])
        backward(c, 0)

    wait_bytes(wanted_landed.at[pl.ds(0, n - 1)], recv_sem.at[meta_index + 1])
    to_scalar = pltpu.make_async_copy(wanted_landed, wanted, local_sem)
    to_scalar.start()
    to_scalar.wait()

    def add_mass(p, sums):
        sums = list(sums)
        for j in range(per):
            mass = meta[p, cols + j : cols + j + 1, :]
            w = wanted[p, 0, j]
            for k in range(cols):
                sums[k] = sums[k] + mass * (w == k).astype(F32)
        return tuple(sums)

    masses = lax.fori_loop(0, n, add_mass, tuple(jnp.zeros((1, blk), F32) for _ in range(cols)))
    for k in range(cols):
        inverse[k : k + 1, :] = 1.0 / masses[k]

    for c in range(chunk_count):
        sums = gather(c, 0)
        for k in range(cols):
            estimate[c * cols + k] = (prior[k : k + 1, :] * inverse[k : k + 1, :]) * sums[k]
        wait_sent(c, 0)
        spread(c)
    for c in range(chunk_count):
        fold(c)
        wait_sent(c, 1)
        backward(c, 2)
    for c in range(chunk_count):
        sums = gather(c, 2)
        for k in range(cols):
            out[c * rc : (c + 1) * rc, k * blk : (k + 1) * blk] = (
                estimate[c * cols + k] * sums[k] * inverse[k : k + 1, :]
            )
        wait_sent(c, 2)
    wait_bytes(message.at[pl.ds(0, n - 1)], send_sem.at[meta_index])
    wait_bytes(wanted_landed.at[pl.ds(0, n - 1)], send_sem.at[meta_index + 1])


def local(response, block_row, block_col, counts, prior):
    n = lax.axis_size("rows")
    slots, blk, _ = response.shape
    per = slots // n
    reps = counts.shape[0]
    rows = counts.shape[1] // blk
    cols = prior.shape[0] // blk
    rc = reps // CHUNKS
    local_col = block_col % cols
    message_rows = -(-(cols + per) // 8) * 8
    col_message = jnp.pad(local_col.reshape(n, 1, per), ((0, 0), (0, 7), (0, blk - per)))
    vmem = pl.BlockSpec(memory_space=pltpu.VMEM)
    smem = pl.BlockSpec(memory_space=pltpu.SMEM)
    sems = 3 * CHUNKS + 2
    return pl.pallas_call(
        functools.partial(kernel, n, per, cols, rows, CHUNKS),
        out_shape=jax.ShapeDtypeStruct((reps, cols * blk), F32),
        in_specs=[vmem, smem, smem, vmem, vmem, vmem],
        out_specs=vmem,
        scratch_shapes=[
            pltpu.VMEM((slots, 2 * blk, blk), BF16),
            pltpu.VMEM((n, message_rows, blk), F32),
            pltpu.VMEM((n, message_rows, blk), F32),
            pltpu.VMEM((n, 8, blk), jnp.int32),
            pltpu.SMEM((n, 8, blk), jnp.int32),
            pltpu.VMEM((CHUNKS, slots, rc, blk), F32),
            pltpu.VMEM((CHUNKS, slots, rc, blk), F32),
            pltpu.VMEM((CHUNKS, slots, rc, blk), F32),
            pltpu.VMEM((CHUNKS * cols, rc, blk), F32),
            pltpu.VMEM((rows * CHUNKS, 2 * rc, blk), BF16),
            pltpu.VMEM((-(-cols // 8) * 8, blk), F32),
            pltpu.SemaphoreType.DMA((sems,)),
            pltpu.SemaphoreType.DMA((sems,)),
            pltpu.SemaphoreType.DMA,
        ],
        compiler_params=pltpu.CompilerParams(
            collective_id=0, has_side_effects=True, vmem_limit_bytes=60 * 1024 * 1024
        ),
    )(response, block_row, local_col, col_message, counts, prior.reshape(cols, blk))


def solution(mesh):
    in_specs = (
        P(("groups", "rows"), None, None),
        P(("groups", "rows")),
        P(("groups", "rows")),
        P(None, ("groups", "rows")),
        P(("groups", "rows")),
    )
    out_specs = P(None, ("groups", "rows"))
    return jax.shard_map(local, mesh=mesh, in_specs=in_specs, out_specs=out_specs, check_vma=False)
```

```python
import functools

import jax
import jax.numpy as jnp
from jax import lax
from jax.experimental import pallas as pl
from jax.experimental.pallas import tpu as pltpu
from jax.sharding import PartitionSpec as P

CHUNKS = 2
KINDS = 9
F32 = jnp.float32
BF16 = jnp.bfloat16
RELAY, NEAR, DENSE, AHEAD, PICK, RELAY_PICK = 0, 1, 2, 6, 7, 8


def split(x):
    high = x.astype(BF16).astype(F32)
    return jnp.concatenate([high, x - high], axis=0).astype(BF16)


def kernel(
    n, per, cols, rows, chunk_count,
    response, block_row, local_col, col_message, counts, prior,
    out,
    response_split, own_prior, priors, mass_message, mass_landed, mass_out, mass_far,
    wanted_landed, wanted, send, relay_in, near_in, dense_out, dense_in, ahead, relayed, fetched, estimate,
    ratio, inverse, send_sem, recv_sem, local_sem,
):
    blk = prior.shape[1]
    half = n // 2
    rc = counts.shape[0] // chunk_count
    me = lax.axis_index("rows")
    side = me // half
    base = side * half
    other = (1 - side) * half
    place = me - base
    partner = other + place

    def near(k):
        return lax.rem(place + k + 1, half)

    def remote(src, dst, index, peer):
        return pltpu.make_async_remote_copy(
            src_ref=src, dst_ref=dst, send_sem=send_sem.at[index], recv_sem=recv_sem.at[index],
            device_id={"rows": peer}, device_id_type=pl.DeviceIdType.MESH,
        )

    def wait_bytes(ref, sem):
        pltpu.make_async_copy(ref, ref, sem).wait()

    def sem_of(c, kind):
        return c * KINDS + kind

    PRIOR, WANTED, MASS, MASS_DENSE = (KINDS * chunk_count + i for i in range(4))
    few = pl.ds(0, (half - 1) * per)

    barrier = pltpu.get_barrier_semaphore()

    @pl.loop(0, n - 1)
    def _(k):
        pl.semaphore_signal(
            barrier, inc=1, device_id={"rows": lax.rem(me + k + 1, n)},
            device_id_type=pl.DeviceIdType.MESH,
        )

    own_prior[...] = jnp.zeros_like(own_prior)
    own_prior[0:cols, :] = prior[...]
    priors[me] = own_prior[...]

    def prepare(i, row, owner):
        for j in range(per):
            block = response[owner * per + j]
            at = row * per + j
            mass_message[i, at : at + 1, :] = jnp.sum(block, axis=0, keepdims=True)
            response_split[owner * per + j] = split(block)

    @pl.loop(0, half)
    def _(i):
        prepare(i, 0, base + i)

    pl.semaphore_wait(barrier, n - 1)

    @pl.loop(0, n - 1)
    def _(k):
        remote(own_prior, priors.at[me], PRIOR, lax.rem(me + k + 1, n)).start()

    @pl.loop(0, half)
    def _(i):
        prepare(i, 1, other + i)

    @pl.loop(0, half - 1)
    def _(k):
        q = near(k)
        remote(col_message.at[q], wanted_landed.at[place], WANTED, base + q).start()
        remote(mass_message.at[q], mass_landed.at[place], MASS, base + q).start()

    wanted_landed[place] = col_message[place]
    mass_landed[place] = mass_message[place]
    wait_bytes(priors.at[pl.ds(0, n - 1)], recv_sem.at[PRIOR])

    def fold_prior(p, total):
        for j in range(per):
            s = p * per + j
            row = priors[p, pl.ds(local_col[s], 1), :]
            spot = lax.broadcasted_iota(jnp.int32, (rows, blk), 0) == block_row[s]
            masked = jnp.where(spot, jnp.broadcast_to(row, (rows, blk)), 0.0)
            total = total + lax.dot_general(
                split(masked), response_split[s], (((1,), (1,)), ((), ())), preferred_element_type=F32
            )
        return total

    total = lax.fori_loop(0, n, fold_prior, jnp.zeros((2 * rows, 2 * blk), F32))
    total = total[:rows] + total[rows:]
    first_fold = total[:, :blk] + total[:, blk:]

    def store_ratio(c, b, folded):
        measured = counts[c * rc : (c + 1) * rc, b * blk : (b + 1) * blk].astype(F32)
        ratio[b * chunk_count + c] = split(measured / folded)

    def backward(c, phase):
        def one(s):
            x = ratio[block_row[s] * chunk_count + c]
            both = jnp.dot(
                jnp.concatenate([x, x], axis=1), response_split[s], preferred_element_type=F32
            )
            return both[:rc] + both[rc:]

        for kind, start, landing in ((RELAY, other, relay_in), (NEAR, base, near_in)):
            offset = per if kind == RELAY else 0

            @pl.loop(0, half - 1)
            def _(k):
                q = near(k)
                at = q * 2 * per + offset
                for j in range(per):
                    send[c, at + j] = one((start + q) * per + j)
                remote(
                    send.at[c, pl.ds(at, per)], landing.at[c, pl.ds(place * per, per)],
                    sem_of(c, phase * 3 + kind), base + q,
                ).start()

            for j in range(per):
                landing[c, place * per + j] = one((start + place) * per + j)

    def wait_sent(c, kinds):
        for kind in kinds:
            wait_bytes(send.at[c, few], send_sem.at[sem_of(c, kind)])

    def column_sums(landing, c, whose):
        def add(i, sums):
            sums = list(sums)
            for j in range(per):
                block = landing[c, i * per + j]
                w = wanted[i, 0, whose * per + j]
                for k in range(cols):
                    sums[k] = sums[k] + block * (w == k).astype(F32)
            return tuple(sums)

        return lax.fori_loop(0, half, add, tuple(jnp.zeros((rc, blk), F32) for _ in range(cols)))

    def relay(c, phase):
        if phase == 1:
            wait_bytes(dense_out.at[c], send_sem.at[sem_of(c, DENSE)])
        wait_bytes(relay_in.at[c, few], recv_sem.at[sem_of(c, phase * 3 + RELAY)])
        sums = column_sums(relay_in, c, 1 - side)
        for k in range(cols):
            dense_out[c, k] = sums[k]
        remote(dense_out.at[c], dense_in.at[c], sem_of(c, phase * 3 + DENSE), partner).start()

    def gather(c, phase):
        wait_bytes(near_in.at[c, few], recv_sem.at[sem_of(c, phase * 3 + NEAR)])
        sums = column_sums(near_in, c, side)
        wait_bytes(dense_in.at[c], recv_sem.at[sem_of(c, phase * 3 + DENSE)])
        return [sums[k] + dense_in[c, k] for k in range(cols)]

    def pick(c, source, whose, owner, offset, kind):
        @pl.loop(0, half - 1)
        def _(k):
            q = near(k)
            at = q * 2 * per + offset
            for j in range(per):
                send[c, at + j] = source[c, wanted[q, 0, whose * per + j]]
            remote(
                send.at[c, pl.ds(at, per)], fetched.at[c, pl.ds(owner * per, per)],
                sem_of(c, kind), base + q,
            ).start()

        for j in range(per):
            fetched[c, owner * per + j] = source[c, wanted[place, 0, whose * per + j]]

    def update(c):
        sums = gather(c, 0)
        for k in range(cols):
            estimate[c, k] = (prior[k : k + 1, :] * inverse[k : k + 1, :]) * sums[k]
        remote(estimate.at[c], ahead.at[c], sem_of(c, AHEAD), partner).start()
        wait_sent(c, (RELAY, NEAR))
        pick(c, estimate, side, me, 0, PICK)

    def relay_pick(c):
        wait_bytes(ahead.at[c], recv_sem.at[sem_of(c, AHEAD)])
        relayed[c] = ahead[c]
        pick(c, relayed, 1 - side, partner, per, RELAY_PICK)

    def fold(c):
        def add(start):
            def body(i, sums):
                sums = list(sums)
                for j in range(per):
                    s = (start + i) * per + j
                    product = lax.dot_general(
                        split(fetched[c, s]), response_split[s], (((1,), (1,)), ((), ())),
                        preferred_element_type=F32,
                    )
                    product = product[:rc] + product[rc:]
                    product = product[:, :blk] + product[:, blk:]
                    r = block_row[s]
                    for b in range(rows):
                        sums[b] = sums[b] + product * (r == b).astype(F32)
                return tuple(sums)

            return body

        sums = tuple(jnp.zeros((rc, blk), F32) for _ in range(rows))
        wait_bytes(fetched.at[c, few], recv_sem.at[sem_of(c, PICK)])
        sums = lax.fori_loop(0, half, add(base), sums)
        wait_bytes(fetched.at[c, few], recv_sem.at[sem_of(c, RELAY_PICK)])
        sums = lax.fori_loop(0, half, add(other), sums)
        for b in range(rows):
            store_ratio(c, b, sums[b])

    def masses():
        wait_bytes(wanted_landed.at[pl.ds(0, half - 1)], recv_sem.at[WANTED])
        to_scalar = pltpu.make_async_copy(wanted_landed, wanted, local_sem)
        to_scalar.start()
        to_scalar.wait()
        wait_bytes(mass_landed.at[pl.ds(0, half - 1)], recv_sem.at[MASS])

        def sums_of(row, whose):
            def add(i, sums):
                sums = list(sums)
                for j in range(per):
                    mass = mass_landed[i, row * per + j : row * per + j + 1, :]
                    w = wanted[i, 0, whose * per + j]
                    for k in range(cols):
                        sums[k] = sums[k] + mass * (w == k).astype(F32)
                return tuple(sums)

            return lax.fori_loop(0, half, add, tuple(jnp.zeros((1, blk), F32) for _ in range(cols)))

        mass_out[...] = jnp.zeros_like(mass_out)
        for k, mass in enumerate(sums_of(1, 1 - side)):
            mass_out[k : k + 1, :] = mass
        remote(mass_out, mass_far, MASS_DENSE, partner).start()
        for k, mass in enumerate(sums_of(0, side)):
            inverse[k : k + 1, :] = mass

    def efficiencies():
        wait_bytes(mass_far, recv_sem.at[MASS_DENSE])
        inverse[0:cols, :] = 1.0 / (inverse[0:cols, :] + mass_far[0:cols, :])

    def first(c):
        for b in range(rows):
            store_ratio(c, b, first_fold[b : b + 1])
        backward(c, 0)

    def second(c):
        fold(c)
        wait_sent(c, (PICK, RELAY_PICK))
        backward(c, 1)

    def finish(c):
        sums = gather(c, 1)
        for k in range(cols):
            out[c * rc : (c + 1) * rc, k * blk : (k + 1) * blk] = (
                estimate[c, k] * sums[k] * inverse[k : k + 1, :]
            )

    chunks = range(chunk_count)
    for c in chunks:
        first(c)
    masses()
    for c in chunks:
        relay(c, 0)
    efficiencies()
    for c in chunks:
        update(c)
    for c in chunks:
        relay_pick(c)
    for c in chunks:
        second(c)
    for c in chunks:
        relay(c, 1)
    for c in chunks:
        finish(c)

    for c in chunks:
        wait_sent(c, (3 + RELAY, 3 + NEAR))
        wait_bytes(dense_out.at[c], send_sem.at[sem_of(c, 3 + DENSE)])
        wait_bytes(estimate.at[c], send_sem.at[sem_of(c, AHEAD)])
    wait_bytes(priors.at[pl.ds(0, n - 1)], send_sem.at[PRIOR])
    wait_bytes(wanted_landed.at[pl.ds(0, half - 1)], send_sem.at[WANTED])
    wait_bytes(mass_landed.at[pl.ds(0, half - 1)], send_sem.at[MASS])
    wait_bytes(mass_out, send_sem.at[MASS_DENSE])


def local(response, block_row, block_col, counts, prior):
    n = lax.axis_size("rows")
    half = n // 2
    slots, blk, _ = response.shape
    per = slots // n
    reps = counts.shape[0]
    rows = counts.shape[1] // blk
    cols = prior.shape[0] // blk
    rc = reps // CHUNKS
    tall = -(-cols // 8) * 8
    mass_rows = -(-2 * per // 8) * 8
    local_col = block_col % cols
    both = local_col.reshape(2, half, per).transpose(1, 0, 2).reshape(half, 1, 2 * per)
    col_message = jnp.pad(both, ((0, 0), (0, 0), (0, blk - 2 * per)))
    vmem = pl.BlockSpec(memory_space=pltpu.VMEM)
    smem = pl.BlockSpec(memory_space=pltpu.SMEM)
    sems = KINDS * CHUNKS + 4
    return pl.pallas_call(
        functools.partial(kernel, n, per, cols, rows, CHUNKS),
        out_shape=jax.ShapeDtypeStruct((reps, cols * blk), F32),
        in_specs=[vmem, smem, smem, vmem, vmem, vmem],
        out_specs=vmem,
        scratch_shapes=[
            pltpu.VMEM((slots, 2 * blk, blk), BF16),
            pltpu.VMEM((tall, blk), F32),
            pltpu.VMEM((n, tall, blk), F32),
            pltpu.VMEM((half, mass_rows, blk), F32),
            pltpu.VMEM((half, mass_rows, blk), F32),
            pltpu.VMEM((tall, blk), F32),
            pltpu.VMEM((tall, blk), F32),
            pltpu.VMEM((half, 1, blk), jnp.int32),
            pltpu.SMEM((half, 1, blk), jnp.int32),
            pltpu.VMEM((CHUNKS, slots, rc, blk), F32),
            pltpu.VMEM((CHUNKS, half * per, rc, blk), F32),
            pltpu.VMEM((CHUNKS, half * per, rc, blk), F32),
            pltpu.VMEM((CHUNKS, cols, rc, blk), F32),
            pltpu.VMEM((CHUNKS, cols, rc, blk), F32),
            pltpu.VMEM((CHUNKS, cols, rc, blk), F32),
            pltpu.VMEM((CHUNKS, cols, rc, blk), F32),
            pltpu.VMEM((CHUNKS, slots, rc, blk), F32),
            pltpu.VMEM((CHUNKS, cols, rc, blk), F32),
            pltpu.VMEM((rows * CHUNKS, 2 * rc, blk), BF16),
            pltpu.VMEM((tall, blk), F32),
            pltpu.SemaphoreType.DMA((sems,)),
            pltpu.SemaphoreType.DMA((sems,)),
            pltpu.SemaphoreType.DMA,
        ],
        compiler_params=pltpu.CompilerParams(
            collective_id=0, has_side_effects=True, vmem_limit_bytes=60 * 1024 * 1024
        ),
    )(response, block_row, local_col, col_message, counts, prior.reshape(cols, blk))


def solution(mesh):
    in_specs = (
        P(("groups", "rows"), None, None),
        P(("groups", "rows")),
        P(("groups", "rows")),
        P(None, ("groups", "rows")),
        P(("groups", "rows")),
    )
    out_specs = P(None, ("groups", "rows"))
    return jax.shard_map(local, mesh=mesh, in_specs=in_specs, out_specs=out_specs, check_vma=False)
```

```python
import functools

import jax
import jax.numpy as jnp
from jax import lax
from jax.experimental import pallas as pl
from jax.experimental.pallas import tpu as pltpu
from jax.sharding import PartitionSpec as P

CHUNKS = 2
KINDS = 9
F32 = jnp.float32
BF16 = jnp.bfloat16
RELAY, NEAR, DENSE, AHEAD, PICK, RELAY_PICK = 0, 1, 2, 6, 7, 8


def split(x):
    high = x.astype(BF16).astype(F32)
    return jnp.concatenate([high, x - high], axis=0).astype(BF16)


def kernel(
    n, per, cols, rows, chunk_count,
    response_hbm, block_row, block_col, counts, prior,
    out,
    response, response_split, col_message, own_prior, priors, mass_message, mass_landed, mass_out, mass_far,
    wanted_landed, wanted, send, relay_in, near_in, dense_out, dense_in, ahead, relayed, fetched, estimate,
    ratio, inverse, send_sem, recv_sem, local_sem, load_sem,
):
    blk = prior.shape[1]
    half = n // 2
    rc = counts.shape[0] // chunk_count
    me = lax.axis_index("rows")
    side = me // half
    base = side * half
    other = (1 - side) * half
    place = me - base
    partner = other + place

    def near(k):
        return lax.rem(place + k + 1, half)

    def load(start, i):
        part = pl.ds(start * per, half * per)
        return pltpu.make_async_copy(response_hbm.at[part], response.at[part], load_sem.at[i])

    load(base, 0).start()
    load(other, 1).start()

    def remote(src, dst, index, peer):
        return pltpu.make_async_remote_copy(
            src_ref=src, dst_ref=dst, send_sem=send_sem.at[index], recv_sem=recv_sem.at[index],
            device_id={"rows": peer}, device_id_type=pl.DeviceIdType.MESH,
        )

    def wait_bytes(ref, sem):
        pltpu.make_async_copy(ref, ref, sem).wait()

    def sem_of(c, kind):
        return c * KINDS + kind

    PRIOR, WANTED, MASS, MASS_DENSE = (KINDS * chunk_count + i for i in range(4))
    few = pl.ds(0, (half - 1) * per)

    barrier = pltpu.get_barrier_semaphore()

    @pl.loop(0, n - 1)
    def _(k):
        pl.semaphore_signal(
            barrier, inc=1, device_id={"rows": lax.rem(me + k + 1, n)},
            device_id_type=pl.DeviceIdType.MESH,
        )

    own_prior[...] = jnp.zeros_like(own_prior)
    own_prior[0:cols, :] = prior[...]
    priors[me] = own_prior[...]

    def prepare(i, row, owner):
        for j in range(per):
            block = response[owner * per + j]
            at = row * per + j
            mass_message[i, at : at + 1, :] = jnp.sum(block, axis=0, keepdims=True)
            response_split[owner * per + j] = split(block)

    pl.semaphore_wait(barrier, n - 1)

    @pl.loop(0, n - 1)
    def _(k):
        remote(own_prior, priors.at[me], PRIOR, lax.rem(me + k + 1, n)).start()

    lane = lax.broadcasted_iota(jnp.int32, (1, blk), 1)

    @pl.loop(0, half)
    def _(i):
        line = jnp.zeros((1, blk), jnp.int32)
        for t in range(2):
            for j in range(per):
                owner = t * half + i
                value = lax.rem(block_col[owner * per + j], cols)
                line = jnp.where(lane == t * per + j, value, line)
        col_message[i] = line

    load(base, 0).wait()

    @pl.loop(0, half)
    def _(i):
        prepare(i, 0, base + i)

    load(other, 1).wait()

    @pl.loop(0, half)
    def _(i):
        prepare(i, 1, other + i)

    @pl.loop(0, half - 1)
    def _(k):
        q = near(k)
        remote(col_message.at[q], wanted_landed.at[place], WANTED, base + q).start()
        remote(mass_message.at[q], mass_landed.at[place], MASS, base + q).start()

    wanted_landed[place] = col_message[place]
    mass_landed[place] = mass_message[place]
    wait_bytes(priors.at[pl.ds(0, n - 1)], recv_sem.at[PRIOR])

    def fold_prior(p, total):
        for j in range(per):
            s = p * per + j
            row = priors[p, pl.ds(lax.rem(block_col[s], cols), 1), :]
            spot = lax.broadcasted_iota(jnp.int32, (rows, blk), 0) == block_row[s]
            masked = jnp.where(spot, jnp.broadcast_to(row, (rows, blk)), 0.0)
            total = total + lax.dot_general(
                split(masked), response_split[s], (((1,), (1,)), ((), ())), preferred_element_type=F32
            )
        return total

    total = lax.fori_loop(0, n, fold_prior, jnp.zeros((2 * rows, 2 * blk), F32), unroll=4)
    total = total[:rows] + total[rows:]
    first_fold = total[:, :blk] + total[:, blk:]

    def store_ratio(c, b, folded):
        measured = counts[c * rc : (c + 1) * rc, b * blk : (b + 1) * blk].astype(F32)
        ratio[b * chunk_count + c] = split(measured / folded)

    def backward(c, phase, kinds=((RELAY, other, relay_in), (NEAR, base, near_in))):
        def one(s):
            x = ratio[block_row[s] * chunk_count + c]
            both = jnp.dot(
                jnp.concatenate([x, x], axis=1), response_split[s], preferred_element_type=F32
            )
            return both[:rc] + both[rc:]

        for kind, start, landing in kinds:
            offset = per if kind == RELAY else 0

            @pl.loop(0, half - 1, unroll=7)
            def _(k):
                q = near(k)
                at = q * 2 * per + offset
                for j in range(per):
                    send[c, at + j] = one((start + q) * per + j)
                remote(
                    send.at[c, pl.ds(at, per)], landing.at[c, pl.ds(place * per, per)],
                    sem_of(c, phase * 3 + kind), base + q,
                ).start()

            for j in range(per):
                landing[c, place * per + j] = one((start + place) * per + j)

    def wait_sent(c, kinds):
        for kind in kinds:
            wait_bytes(send.at[c, few], send_sem.at[sem_of(c, kind)])

    def column_sums(landing, c, whose):
        def add(i, sums):
            sums = list(sums)
            for j in range(per):
                block = landing[c, i * per + j]
                w = wanted[i, 0, whose * per + j]
                for k in range(cols):
                    sums[k] = sums[k] + block * (w == k).astype(F32)
            return tuple(sums)

        return lax.fori_loop(0, half, add, tuple(jnp.zeros((rc, blk), F32) for _ in range(cols)))

    def relay(c, phase):
        if phase == 1:
            wait_bytes(dense_out.at[c], send_sem.at[sem_of(c, DENSE)])
        wait_bytes(relay_in.at[c, few], recv_sem.at[sem_of(c, phase * 3 + RELAY)])
        sums = column_sums(relay_in, c, 1 - side)
        for k in range(cols):
            dense_out[c, k] = sums[k]
        remote(dense_out.at[c], dense_in.at[c], sem_of(c, phase * 3 + DENSE), partner).start()

    def gather(c, phase):
        wait_bytes(near_in.at[c, few], recv_sem.at[sem_of(c, phase * 3 + NEAR)])
        sums = column_sums(near_in, c, side)
        wait_bytes(dense_in.at[c], recv_sem.at[sem_of(c, phase * 3 + DENSE)])
        return [sums[k] + dense_in[c, k] for k in range(cols)]

    def pick(c, source, whose, owner, offset, kind):
        @pl.loop(0, half - 1)
        def _(k):
            q = near(k)
            at = q * 2 * per + offset
            for j in range(per):
                send[c, at + j] = source[c, wanted[q, 0, whose * per + j]]
            remote(
                send.at[c, pl.ds(at, per)], fetched.at[c, pl.ds(owner * per, per)],
                sem_of(c, kind), base + q,
            ).start()

        for j in range(per):
            fetched[c, owner * per + j] = source[c, wanted[place, 0, whose * per + j]]

    def update(c):
        sums = gather(c, 0)
        for k in range(cols):
            estimate[c, k] = (prior[k : k + 1, :] * inverse[k : k + 1, :]) * sums[k]
        remote(estimate.at[c], ahead.at[c], sem_of(c, AHEAD), partner).start()
        wait_sent(c, (RELAY, NEAR))
        pick(c, estimate, side, me, 0, PICK)

    def relay_pick(c):
        wait_bytes(ahead.at[c], recv_sem.at[sem_of(c, AHEAD)])
        relayed[c] = ahead[c]
        pick(c, relayed, 1 - side, partner, per, RELAY_PICK)

    def fold(c):
        def add(start):
            def body(i, sums):
                sums = list(sums)
                for j in range(per):
                    s = (start + i) * per + j
                    product = lax.dot_general(
                        split(fetched[c, s]), response_split[s], (((1,), (1,)), ((), ())),
                        preferred_element_type=F32,
                    )
                    product = product[:rc] + product[rc:]
                    product = product[:, :blk] + product[:, blk:]
                    r = block_row[s]
                    for b in range(rows):
                        sums[b] = sums[b] + product * (r == b).astype(F32)
                return tuple(sums)

            return body

        sums = tuple(jnp.zeros((rc, blk), F32) for _ in range(rows))
        wait_bytes(fetched.at[c, few], recv_sem.at[sem_of(c, PICK)])
        sums = lax.fori_loop(0, half, add(base), sums, unroll=4)
        wait_bytes(fetched.at[c, few], recv_sem.at[sem_of(c, RELAY_PICK)])
        sums = lax.fori_loop(0, half, add(other), sums, unroll=4)
        for b in range(rows):
            store_ratio(c, b, sums[b])

    def masses():
        wait_bytes(wanted_landed.at[pl.ds(0, half - 1)], recv_sem.at[WANTED])
        to_scalar = pltpu.make_async_copy(wanted_landed, wanted, local_sem)
        to_scalar.start()
        to_scalar.wait()
        wait_bytes(mass_landed.at[pl.ds(0, half - 1)], recv_sem.at[MASS])

        def sums_of(row, whose):
            def add(i, sums):
                sums = list(sums)
                for j in range(per):
                    mass = mass_landed[i, row * per + j : row * per + j + 1, :]
                    w = wanted[i, 0, whose * per + j]
                    for k in range(cols):
                        sums[k] = sums[k] + mass * (w == k).astype(F32)
                return tuple(sums)

            return lax.fori_loop(0, half, add, tuple(jnp.zeros((1, blk), F32) for _ in range(cols)))

        mass_out[...] = jnp.zeros_like(mass_out)
        for k, mass in enumerate(sums_of(1, 1 - side)):
            mass_out[k : k + 1, :] = mass
        remote(mass_out, mass_far, MASS_DENSE, partner).start()
        for k, mass in enumerate(sums_of(0, side)):
            inverse[k : k + 1, :] = mass

    def efficiencies():
        wait_bytes(mass_far, recv_sem.at[MASS_DENSE])
        inverse[0:cols, :] = 1.0 / (inverse[0:cols, :] + mass_far[0:cols, :])

    def first(c):
        for b in range(rows):
            store_ratio(c, b, first_fold[b : b + 1])
        backward(c, 0)

    def second(c):
        fold(c)
        wait_sent(c, (PICK, RELAY_PICK))
        backward(c, 1)

    def finish(c):
        sums = gather(c, 1)
        for k in range(cols):
            out[c * rc : (c + 1) * rc, k * blk : (k + 1) * blk] = (
                estimate[c, k] * sums[k] * inverse[k : k + 1, :]
            )

    chunks = range(chunk_count)
    for c in chunks:
        for b in range(rows):
            store_ratio(c, b, first_fold[b : b + 1])
        backward(c, 0, ((RELAY, other, relay_in),))
    for c in chunks:
        backward(c, 0, ((NEAR, base, near_in),))
    masses()
    for c in chunks:
        relay(c, 0)
    efficiencies()
    for c in chunks:
        update(c)
    for c in chunks:
        relay_pick(c)
    for c in chunks:
        second(c)
        relay(c, 1)
    for c in chunks:
        finish(c)

    for c in chunks:
        wait_sent(c, (3 + RELAY, 3 + NEAR))
        wait_bytes(dense_out.at[c], send_sem.at[sem_of(c, 3 + DENSE)])
        wait_bytes(estimate.at[c], send_sem.at[sem_of(c, AHEAD)])
    wait_bytes(priors.at[pl.ds(0, n - 1)], send_sem.at[PRIOR])
    wait_bytes(wanted_landed.at[pl.ds(0, half - 1)], send_sem.at[WANTED])
    wait_bytes(mass_landed.at[pl.ds(0, half - 1)], send_sem.at[MASS])
    wait_bytes(mass_out, send_sem.at[MASS_DENSE])


def local(response, block_row, block_col, counts, prior):
    n = lax.axis_size("rows")
    half = n // 2
    slots, blk, _ = response.shape
    per = slots // n
    reps = counts.shape[0]
    rows = counts.shape[1] // blk
    cols = prior.shape[0] // blk
    rc = reps // CHUNKS
    tall = -(-cols // 8) * 8
    mass_rows = -(-2 * per // 8) * 8
    vmem = pl.BlockSpec(memory_space=pltpu.VMEM)
    smem = pl.BlockSpec(memory_space=pltpu.SMEM)
    sems = KINDS * CHUNKS + 4
    return pl.pallas_call(
        functools.partial(kernel, n, per, cols, rows, CHUNKS),
        out_shape=jax.ShapeDtypeStruct((reps, cols * blk), F32),
        in_specs=[pl.BlockSpec(memory_space=pl.ANY), smem, smem, vmem, vmem],
        out_specs=vmem,
        scratch_shapes=[
            pltpu.VMEM((slots, blk, blk), F32),
            pltpu.VMEM((slots, 2 * blk, blk), BF16),
            pltpu.VMEM((half, 1, blk), jnp.int32),
            pltpu.VMEM((tall, blk), F32),
            pltpu.VMEM((n, tall, blk), F32),
            pltpu.VMEM((half, mass_rows, blk), F32),
            pltpu.VMEM((half, mass_rows, blk), F32),
            pltpu.VMEM((tall, blk), F32),
            pltpu.VMEM((tall, blk), F32),
            pltpu.VMEM((half, 1, blk), jnp.int32),
            pltpu.SMEM((half, 1, blk), jnp.int32),
            pltpu.VMEM((CHUNKS, slots, rc, blk), F32),
            pltpu.VMEM((CHUNKS, half * per, rc, blk), F32),
            pltpu.VMEM((CHUNKS, half * per, rc, blk), F32),
            pltpu.VMEM((CHUNKS, cols, rc, blk), F32),
            pltpu.VMEM((CHUNKS, cols, rc, blk), F32),
            pltpu.VMEM((CHUNKS, cols, rc, blk), F32),
            pltpu.VMEM((CHUNKS, cols, rc, blk), F32),
            pltpu.VMEM((CHUNKS, slots, rc, blk), F32),
            pltpu.VMEM((CHUNKS, cols, rc, blk), F32),
            pltpu.VMEM((rows * CHUNKS, 2 * rc, blk), BF16),
            pltpu.VMEM((tall, blk), F32),
            pltpu.SemaphoreType.DMA((sems,)),
            pltpu.SemaphoreType.DMA((sems,)),
            pltpu.SemaphoreType.DMA,
            pltpu.SemaphoreType.DMA((2,)),
        ],
        compiler_params=pltpu.CompilerParams(
            collective_id=0, has_side_effects=True, vmem_limit_bytes=60 * 1024 * 1024
        ),
    )(response, block_row, block_col, counts, prior.reshape(cols, blk))


def solution(mesh):
    in_specs = (
        P(("groups", "rows"), None, None),
        P(("groups", "rows")),
        P(("groups", "rows")),
        P(None, ("groups", "rows")),
        P(("groups", "rows")),
    )
    out_specs = P(None, ("groups", "rows"))
    return jax.shard_map(local, mesh=mesh, in_specs=in_specs, out_specs=out_specs, check_vma=False)
```

```python
import functools

import jax
import jax.numpy as jnp
from jax import lax
from jax.experimental import pallas as pl
from jax.experimental.pallas import tpu as pltpu
from jax.sharding import PartitionSpec as P

CHUNKS = 2
KINDS = 9
F32 = jnp.float32
BF16 = jnp.bfloat16
RELAY, NEAR, DENSE, AHEAD, PICK, RELAY_PICK = 0, 1, 2, 6, 7, 8


def split(x):
    high = x.astype(BF16).astype(F32)
    return jnp.concatenate([high, x - high], axis=0).astype(BF16)


def kernel(
    n, per, cols, rows, chunk_count,
    response_hbm, block_row, block_col, counts, prior,
    out,
    response, response_split, col_message, own_prior, priors, mass_message, mass_landed, mass_out, mass_far,
    wanted_landed, wanted, send, relay_in, near_in, dense_out, dense_in, ahead, relayed, fetched, estimate,
    ratio, inverse, send_sem, recv_sem, local_sem, load_sem,
):
    blk = prior.shape[1]
    half = n // 2
    rc = counts.shape[0] // chunk_count
    me = lax.axis_index("rows")
    side = me // half
    base = side * half
    other = (1 - side) * half
    place = me - base
    partner = other + place

    def near(k):
        return lax.rem(place + k + 1, half)

    def load(start, i):
        part = pl.ds(start * per, half * per)
        return pltpu.make_async_copy(response_hbm.at[part], response.at[part], load_sem.at[i])

    load(base, 0).start()
    load(other, 1).start()

    def remote(src, dst, index, peer):
        return pltpu.make_async_remote_copy(
            src_ref=src, dst_ref=dst, send_sem=send_sem.at[index], recv_sem=recv_sem.at[index],
            device_id={"rows": peer}, device_id_type=pl.DeviceIdType.MESH,
        )

    def wait_bytes(ref, sem):
        pltpu.make_async_copy(ref, ref, sem).wait()

    def sem_of(c, kind):
        return c * KINDS + kind

    PRIOR, WANTED, MASS, MASS_DENSE = (KINDS * chunk_count + i for i in range(4))
    few = pl.ds(0, (half - 1) * per)

    barrier = pltpu.get_barrier_semaphore()

    @pl.loop(0, n - 1)
    def _(k):
        pl.semaphore_signal(
            barrier, inc=1, device_id={"rows": lax.rem(me + k + 1, n)},
            device_id_type=pl.DeviceIdType.MESH,
        )

    own_prior[...] = jnp.zeros_like(own_prior)
    own_prior[0:cols, :] = prior[...]
    priors[me] = own_prior[...]

    def prepare(i, row, owner):
        for j in range(per):
            block = response[owner * per + j]
            at = row * per + j
            mass_message[i, at : at + 1, :] = jnp.sum(block, axis=0, keepdims=True)
            response_split[owner * per + j] = split(block)

    pl.semaphore_wait(barrier, n - 1)

    @pl.loop(0, n - 1)
    def _(k):
        remote(own_prior, priors.at[me], PRIOR, lax.rem(me + k + 1, n)).start()

    lane = lax.broadcasted_iota(jnp.int32, (1, blk), 1)

    @pl.loop(0, half)
    def _(i):
        line = jnp.zeros((1, blk), jnp.int32)
        for t in range(2):
            for j in range(per):
                owner = t * half + i
                value = lax.rem(block_col[owner * per + j], cols)
                line = jnp.where(lane == t * per + j, value, line)
        col_message[i] = line

    load(base, 0).wait()

    @pl.loop(0, half)
    def _(i):
        prepare(i, 0, base + i)

    load(other, 1).wait()

    @pl.loop(0, half)
    def _(i):
        prepare(i, 1, other + i)

    @pl.loop(0, half - 1)
    def _(k):
        q = near(k)
        remote(col_message.at[q], wanted_landed.at[place], WANTED, base + q).start()
        remote(mass_message.at[q], mass_landed.at[place], MASS, base + q).start()

    wanted_landed[place] = col_message[place]
    mass_landed[place] = mass_message[place]
    wait_bytes(priors.at[pl.ds(0, n - 1)], recv_sem.at[PRIOR])

    def fold_prior(p, total):
        for j in range(per):
            s = p * per + j
            row = priors[p, pl.ds(lax.rem(block_col[s], cols), 1), :]
            spot = lax.broadcasted_iota(jnp.int32, (rows, blk), 0) == block_row[s]
            masked = jnp.where(spot, jnp.broadcast_to(row, (rows, blk)), 0.0)
            total = total + lax.dot_general(
                split(masked), response_split[s], (((1,), (1,)), ((), ())), preferred_element_type=F32
            )
        return total

    total = lax.fori_loop(0, n, fold_prior, jnp.zeros((2 * rows, 2 * blk), F32), unroll=4)
    total = total[:rows] + total[rows:]
    first_fold = total[:, :blk] + total[:, blk:]

    def store_ratio(c, b, folded):
        measured = counts[c * rc : (c + 1) * rc, b * blk : (b + 1) * blk].astype(F32)
        ratio[b * chunk_count + c] = split(measured / folded)

    def backward(c, phase, kinds=((RELAY, other, relay_in), (NEAR, base, near_in))):
        def one(s):
            x = ratio[block_row[s] * chunk_count + c]
            both = jnp.dot(
                jnp.concatenate([x, x], axis=1), response_split[s], preferred_element_type=F32
            )
            return both[:rc] + both[rc:]

        for kind, start, landing in kinds:
            offset = per if kind == RELAY else 0

            @pl.loop(0, half - 1, unroll=7)
            def _(k):
                q = near(k)
                at = q * 2 * per + offset
                for j in range(per):
                    send[c, at + j] = one((start + q) * per + j)
                remote(
                    send.at[c, pl.ds(at, per)], landing.at[c, pl.ds(place * per, per)],
                    sem_of(c, phase * 3 + kind), base + q,
                ).start()

            for j in range(per):
                landing[c, place * per + j] = one((start + place) * per + j)

    def wait_sent(c, kinds):
        for kind in kinds:
            wait_bytes(send.at[c, few], send_sem.at[sem_of(c, kind)])

    def column_sums(landing, c, whose):
        def add(i, sums):
            sums = list(sums)
            for j in range(per):
                block = landing[c, i * per + j]
                w = wanted[i, 0, whose * per + j]
                for k in range(cols):
                    sums[k] = sums[k] + block * (w == k).astype(F32)
            return tuple(sums)

        return lax.fori_loop(0, half, add, tuple(jnp.zeros((rc, blk), F32) for _ in range(cols)))

    def relay(c, phase):
        if phase == 1:
            wait_bytes(dense_out.at[c], send_sem.at[sem_of(c, DENSE)])
        wait_bytes(relay_in.at[c, few], recv_sem.at[sem_of(c, phase * 3 + RELAY)])
        sums = column_sums(relay_in, c, 1 - side)
        for k in range(cols):
            dense_out[c, k] = sums[k]
        remote(dense_out.at[c], dense_in.at[c], sem_of(c, phase * 3 + DENSE), partner).start()

    def gather(c, phase):
        wait_bytes(near_in.at[c, few], recv_sem.at[sem_of(c, phase * 3 + NEAR)])
        sums = column_sums(near_in, c, side)
        wait_bytes(dense_in.at[c], recv_sem.at[sem_of(c, phase * 3 + DENSE)])
        return [sums[k] + dense_in[c, k] for k in range(cols)]

    def pick(c, source, whose, owner, offset, kind):
        @pl.loop(0, half - 1)
        def _(k):
            q = near(k)
            at = q * 2 * per + offset
            for j in range(per):
                send[c, at + j] = source[c, wanted[q, 0, whose * per + j]]
            remote(
                send.at[c, pl.ds(at, per)], fetched.at[c, pl.ds(owner * per, per)],
                sem_of(c, kind), base + q,
            ).start()

        for j in range(per):
            fetched[c, owner * per + j] = source[c, wanted[place, 0, whose * per + j]]

    def update(c):
        sums = gather(c, 0)
        for k in range(cols):
            estimate[c, k] = (prior[k : k + 1, :] * inverse[k : k + 1, :]) * sums[k]
        remote(estimate.at[c], ahead.at[c], sem_of(c, AHEAD), partner).start()
        wait_sent(c, (RELAY, NEAR))
        pick(c, estimate, side, me, 0, PICK)

    def relay_pick(c):
        wait_bytes(ahead.at[c], recv_sem.at[sem_of(c, AHEAD)])
        relayed[c] = ahead[c]
        pick(c, relayed, 1 - side, partner, per, RELAY_PICK)

    def fold(c):
        def add(start):
            def body(i, sums):
                sums = list(sums)
                for j in range(per):
                    s = (start + i) * per + j
                    product = lax.dot_general(
                        split(fetched[c, s]), response_split[s], (((1,), (1,)), ((), ())),
                        preferred_element_type=F32,
                    )
                    product = product[:rc] + product[rc:]
                    product = product[:, :blk] + product[:, blk:]
                    r = block_row[s]
                    for b in range(rows):
                        sums[b] = sums[b] + product * (r == b).astype(F32)
                return tuple(sums)

            return body

        sums = tuple(jnp.zeros((rc, blk), F32) for _ in range(rows))
        wait_bytes(fetched.at[c, few], recv_sem.at[sem_of(c, PICK)])
        sums = lax.fori_loop(0, half, add(base), sums, unroll=4)
        wait_bytes(fetched.at[c, few], recv_sem.at[sem_of(c, RELAY_PICK)])
        sums = lax.fori_loop(0, half, add(other), sums, unroll=4)
        for b in range(rows):
            store_ratio(c, b, sums[b])

    def masses():
        wait_bytes(wanted_landed.at[pl.ds(0, half - 1)], recv_sem.at[WANTED])
        to_scalar = pltpu.make_async_copy(wanted_landed, wanted, local_sem)
        to_scalar.start()
        to_scalar.wait()
        wait_bytes(mass_landed.at[pl.ds(0, half - 1)], recv_sem.at[MASS])

        def sums_of(row, whose):
            def add(i, sums):
                sums = list(sums)
                for j in range(per):
                    mass = mass_landed[i, row * per + j : row * per + j + 1, :]
                    w = wanted[i, 0, whose * per + j]
                    for k in range(cols):
                        sums[k] = sums[k] + mass * (w == k).astype(F32)
                return tuple(sums)

            return lax.fori_loop(0, half, add, tuple(jnp.zeros((1, blk), F32) for _ in range(cols)))

        mass_out[...] = jnp.zeros_like(mass_out)
        for k, mass in enumerate(sums_of(1, 1 - side)):
            mass_out[k : k + 1, :] = mass
        remote(mass_out, mass_far, MASS_DENSE, partner).start()
        for k, mass in enumerate(sums_of(0, side)):
            inverse[k : k + 1, :] = mass

    def efficiencies():
        wait_bytes(mass_far, recv_sem.at[MASS_DENSE])
        inverse[0:cols, :] = 1.0 / (inverse[0:cols, :] + mass_far[0:cols, :])

    def finish(c):
        sums = gather(c, 1)
        for k in range(cols):
            out[c * rc : (c + 1) * rc, k * blk : (k + 1) * blk] = (
                estimate[c, k] * sums[k] * inverse[k : k + 1, :]
            )

    chunks = range(chunk_count)
    for c in chunks:
        for b in range(rows):
            store_ratio(c, b, first_fold[b : b + 1])
        backward(c, 0, ((RELAY, other, relay_in),))
    for c in chunks:
        backward(c, 0, ((NEAR, base, near_in),))
    masses()
    for c in chunks:
        relay(c, 0)
    efficiencies()
    for c in chunks:
        update(c)
    for c in chunks:
        relay_pick(c)
    for c in chunks:
        fold(c)
        wait_sent(c, (PICK, RELAY_PICK))
        backward(c, 1, ((RELAY, other, relay_in),))
    for c in chunks:
        relay(c, 1)
        backward(c, 1, ((NEAR, base, near_in),))
    for c in chunks:
        finish(c)

    for c in chunks:
        wait_sent(c, (3 + RELAY, 3 + NEAR))
        wait_bytes(dense_out.at[c], send_sem.at[sem_of(c, 3 + DENSE)])
        wait_bytes(estimate.at[c], send_sem.at[sem_of(c, AHEAD)])
    wait_bytes(priors.at[pl.ds(0, n - 1)], send_sem.at[PRIOR])
    wait_bytes(wanted_landed.at[pl.ds(0, half - 1)], send_sem.at[WANTED])
    wait_bytes(mass_landed.at[pl.ds(0, half - 1)], send_sem.at[MASS])
    wait_bytes(mass_out, send_sem.at[MASS_DENSE])


def local(response, block_row, block_col, counts, prior):
    n = lax.axis_size("rows")
    half = n // 2
    slots, blk, _ = response.shape
    per = slots // n
    reps = counts.shape[0]
    rows = counts.shape[1] // blk
    cols = prior.shape[0] // blk
    rc = reps // CHUNKS
    tall = -(-cols // 8) * 8
    mass_rows = -(-2 * per // 8) * 8
    vmem = pl.BlockSpec(memory_space=pltpu.VMEM)
    smem = pl.BlockSpec(memory_space=pltpu.SMEM)
    sems = KINDS * CHUNKS + 4
    return pl.pallas_call(
        functools.partial(kernel, n, per, cols, rows, CHUNKS),
        out_shape=jax.ShapeDtypeStruct((reps, cols * blk), F32),
        in_specs=[pl.BlockSpec(memory_space=pl.ANY), smem, smem, vmem, vmem],
        out_specs=vmem,
        scratch_shapes=[
            pltpu.VMEM((slots, blk, blk), F32),
            pltpu.VMEM((slots, 2 * blk, blk), BF16),
            pltpu.VMEM((half, 1, blk), jnp.int32),
            pltpu.VMEM((tall, blk), F32),
            pltpu.VMEM((n, tall, blk), F32),
            pltpu.VMEM((half, mass_rows, blk), F32),
            pltpu.VMEM((half, mass_rows, blk), F32),
            pltpu.VMEM((tall, blk), F32),
            pltpu.VMEM((tall, blk), F32),
            pltpu.VMEM((half, 1, blk), jnp.int32),
            pltpu.SMEM((half, 1, blk), jnp.int32),
            pltpu.VMEM((CHUNKS, slots, rc, blk), F32),
            pltpu.VMEM((CHUNKS, half * per, rc, blk), F32),
            pltpu.VMEM((CHUNKS, half * per, rc, blk), F32),
            pltpu.VMEM((CHUNKS, cols, rc, blk), F32),
            pltpu.VMEM((CHUNKS, cols, rc, blk), F32),
            pltpu.VMEM((CHUNKS, cols, rc, blk), F32),
            pltpu.VMEM((CHUNKS, cols, rc, blk), F32),
            pltpu.VMEM((CHUNKS, slots, rc, blk), F32),
            pltpu.VMEM((CHUNKS, cols, rc, blk), F32),
            pltpu.VMEM((rows * CHUNKS, 2 * rc, blk), BF16),
            pltpu.VMEM((tall, blk), F32),
            pltpu.SemaphoreType.DMA((sems,)),
            pltpu.SemaphoreType.DMA((sems,)),
            pltpu.SemaphoreType.DMA,
            pltpu.SemaphoreType.DMA((2,)),
        ],
        compiler_params=pltpu.CompilerParams(
            collective_id=0, has_side_effects=True, vmem_limit_bytes=60 * 1024 * 1024
        ),
    )(response, block_row, block_col, counts, prior.reshape(cols, blk))


def solution(mesh):
    in_specs = (
        P(("groups", "rows"), None, None),
        P(("groups", "rows")),
        P(("groups", "rows")),
        P(None, ("groups", "rows")),
        P(("groups", "rows")),
    )
    out_specs = P(None, ("groups", "rows"))
    return jax.shard_map(local, mesh=mesh, in_specs=in_specs, out_specs=out_specs, check_vma=False)
```

```python
import functools

import jax
import jax.numpy as jnp
from jax import lax
from jax.experimental import pallas as pl
from jax.experimental.pallas import tpu as pltpu
from jax.sharding import PartitionSpec as P

CHUNKS = 2
KINDS = 9
F32 = jnp.float32
BF16 = jnp.bfloat16
RELAY, NEAR, DENSE, AHEAD, PICK, RELAY_PICK = 0, 1, 2, 6, 7, 8


def split(x):
    high = x.astype(BF16).astype(F32)
    return jnp.concatenate([high, x - high], axis=0).astype(BF16)


def kernel(
    n, per, cols, rows, chunk_count,
    response_hbm, block_row, block_col, counts_hbm, prior,
    out,
    counts, response, response_split, col_message, own_prior, priors, mass_message, mass_landed, mass_out, mass_far,
    wanted_landed, wanted, send, relay_in, near_in, dense_out, dense_in, ahead, relayed, fetched, estimate,
    ratio, inverse, send_sem, recv_sem, local_sem, load_sem,
):
    blk = prior.shape[1]
    half = n // 2
    rc = counts.shape[0] // chunk_count
    me = lax.axis_index("rows")
    side = me // half
    base = side * half
    other = (1 - side) * half
    place = me - base
    partner = other + place

    def near(k):
        return lax.rem(place + k + 1, half)

    def load(start, i):
        part = pl.ds(start * per, half * per)
        return pltpu.make_async_copy(response_hbm.at[part], response.at[part], load_sem.at[i])

    load(base, 0).start()
    load(other, 1).start()
    load_counts = pltpu.make_async_copy(counts_hbm, counts, load_sem.at[2])
    load_counts.start()

    def remote(src, dst, index, peer):
        return pltpu.make_async_remote_copy(
            src_ref=src, dst_ref=dst, send_sem=send_sem.at[index], recv_sem=recv_sem.at[index],
            device_id={"rows": peer}, device_id_type=pl.DeviceIdType.MESH,
        )

    def wait_bytes(ref, sem):
        pltpu.make_async_copy(ref, ref, sem).wait()

    def sem_of(c, kind):
        return c * KINDS + kind

    PRIOR, WANTED, MASS, MASS_DENSE = (KINDS * chunk_count + i for i in range(4))
    few = pl.ds(0, (half - 1) * per)

    barrier = pltpu.get_barrier_semaphore()

    @pl.loop(0, n - 1)
    def _(k):
        pl.semaphore_signal(
            barrier, inc=1, device_id={"rows": lax.rem(me + k + 1, n)},
            device_id_type=pl.DeviceIdType.MESH,
        )

    own_prior[...] = jnp.zeros_like(own_prior)
    own_prior[0:cols, :] = prior[...]
    priors[me] = own_prior[...]

    def prepare(i, row, owner):
        for j in range(per):
            block = response[owner * per + j]
            at = row * per + j
            mass_message[i, at : at + 1, :] = jnp.sum(block, axis=0, keepdims=True)
            response_split[owner * per + j] = split(block)

    pl.semaphore_wait(barrier, n - 1)

    @pl.loop(0, n - 1)
    def _(k):
        remote(own_prior, priors.at[me], PRIOR, lax.rem(me + k + 1, n)).start()

    lane = lax.broadcasted_iota(jnp.int32, (1, blk), 1)

    @pl.loop(0, half)
    def _(i):
        line = jnp.zeros((1, blk), jnp.int32)
        for t in range(2):
            for j in range(per):
                owner = t * half + i
                value = lax.rem(block_col[owner * per + j], cols)
                line = jnp.where(lane == t * per + j, value, line)
        col_message[i] = line

    load(base, 0).wait()

    @pl.loop(0, half)
    def _(i):
        prepare(i, 0, base + i)

    load(other, 1).wait()

    @pl.loop(0, half)
    def _(i):
        prepare(i, 1, other + i)

    @pl.loop(0, half - 1)
    def _(k):
        q = near(k)
        remote(col_message.at[q], wanted_landed.at[place], WANTED, base + q).start()
        remote(mass_message.at[q], mass_landed.at[place], MASS, base + q).start()

    wanted_landed[place] = col_message[place]
    mass_landed[place] = mass_message[place]
    wait_bytes(priors.at[pl.ds(0, n - 1)], recv_sem.at[PRIOR])

    def fold_prior(p, total):
        for j in range(per):
            s = p * per + j
            row = priors[p, pl.ds(lax.rem(block_col[s], cols), 1), :]
            spot = lax.broadcasted_iota(jnp.int32, (rows, blk), 0) == block_row[s]
            masked = jnp.where(spot, jnp.broadcast_to(row, (rows, blk)), 0.0)
            total = total + lax.dot_general(
                split(masked), response_split[s], (((1,), (1,)), ((), ())), preferred_element_type=F32
            )
        return total

    total = lax.fori_loop(0, n, fold_prior, jnp.zeros((2 * rows, 2 * blk), F32), unroll=4)
    total = total[:rows] + total[rows:]
    first_fold = total[:, :blk] + total[:, blk:]
    load_counts.wait()

    def store_ratio(c, b, folded):
        measured = counts[c * rc : (c + 1) * rc, b * blk : (b + 1) * blk].astype(F32)
        ratio[b * chunk_count + c] = split(measured / folded)

    def backward(c, phase, kinds=((RELAY, other, relay_in), (NEAR, base, near_in))):
        def one(s):
            x = ratio[block_row[s] * chunk_count + c]
            both = jnp.dot(
                jnp.concatenate([x, x], axis=1), response_split[s], preferred_element_type=F32
            )
            return both[:rc] + both[rc:]

        for kind, start, landing in kinds:
            offset = per if kind == RELAY else 0

            @pl.loop(0, half - 1, unroll=7)
            def _(k):
                q = near(k)
                at = q * 2 * per + offset
                for j in range(per):
                    send[c, at + j] = one((start + q) * per + j)
                remote(
                    send.at[c, pl.ds(at, per)], landing.at[c, pl.ds(place * per, per)],
                    sem_of(c, phase * 3 + kind), base + q,
                ).start()

            for j in range(per):
                landing[c, place * per + j] = one((start + place) * per + j)

    def wait_sent(c, kinds):
        for kind in kinds:
            wait_bytes(send.at[c, few], send_sem.at[sem_of(c, kind)])

    def column_sums(landing, c, whose):
        def add(i, sums):
            sums = list(sums)
            for j in range(per):
                block = landing[c, i * per + j]
                w = wanted[i, 0, whose * per + j]
                for k in range(cols):
                    sums[k] = sums[k] + block * (w == k).astype(F32)
            return tuple(sums)

        return lax.fori_loop(0, half, add, tuple(jnp.zeros((rc, blk), F32) for _ in range(cols)))

    def relay(c, phase):
        if phase == 1:
            wait_bytes(dense_out.at[c], send_sem.at[sem_of(c, DENSE)])
        wait_bytes(relay_in.at[c, few], recv_sem.at[sem_of(c, phase * 3 + RELAY)])
        sums = column_sums(relay_in, c, 1 - side)
        for k in range(cols):
            dense_out[c, k] = sums[k]
        remote(dense_out.at[c], dense_in.at[c], sem_of(c, phase * 3 + DENSE), partner).start()

    def gather(c, phase):
        wait_bytes(near_in.at[c, few], recv_sem.at[sem_of(c, phase * 3 + NEAR)])
        sums = column_sums(near_in, c, side)
        wait_bytes(dense_in.at[c], recv_sem.at[sem_of(c, phase * 3 + DENSE)])
        return [sums[k] + dense_in[c, k] for k in range(cols)]

    def pick(c, source, whose, owner, offset, kind):
        @pl.loop(0, half - 1)
        def _(k):
            q = near(k)
            at = q * 2 * per + offset
            for j in range(per):
                send[c, at + j] = source[c, wanted[q, 0, whose * per + j]]
            remote(
                send.at[c, pl.ds(at, per)], fetched.at[c, pl.ds(owner * per, per)],
                sem_of(c, kind), base + q,
            ).start()

        for j in range(per):
            fetched[c, owner * per + j] = source[c, wanted[place, 0, whose * per + j]]

    def update(c):
        sums = gather(c, 0)
        for k in range(cols):
            estimate[c, k] = (prior[k : k + 1, :] * inverse[k : k + 1, :]) * sums[k]
        remote(estimate.at[c], ahead.at[c], sem_of(c, AHEAD), partner).start()
        wait_sent(c, (RELAY, NEAR))
        pick(c, estimate, side, me, 0, PICK)

    def relay_pick(c):
        wait_bytes(ahead.at[c], recv_sem.at[sem_of(c, AHEAD)])
        relayed[c] = ahead[c]
        pick(c, relayed, 1 - side, partner, per, RELAY_PICK)

    def fold(c):
        def add(start):
            def body(i, sums):
                sums = list(sums)
                for j in range(per):
                    s = (start + i) * per + j
                    product = lax.dot_general(
                        split(fetched[c, s]), response_split[s], (((1,), (1,)), ((), ())),
                        preferred_element_type=F32,
                    )
                    product = product[:rc] + product[rc:]
                    product = product[:, :blk] + product[:, blk:]
                    r = block_row[s]
                    for b in range(rows):
                        sums[b] = sums[b] + product * (r == b).astype(F32)
                return tuple(sums)

            return body

        sums = tuple(jnp.zeros((rc, blk), F32) for _ in range(rows))
        wait_bytes(fetched.at[c, few], recv_sem.at[sem_of(c, PICK)])
        sums = lax.fori_loop(0, half, add(base), sums, unroll=4)
        wait_bytes(fetched.at[c, few], recv_sem.at[sem_of(c, RELAY_PICK)])
        sums = lax.fori_loop(0, half, add(other), sums, unroll=4)
        for b in range(rows):
            store_ratio(c, b, sums[b])

    def masses():
        wait_bytes(wanted_landed.at[pl.ds(0, half - 1)], recv_sem.at[WANTED])
        to_scalar = pltpu.make_async_copy(wanted_landed, wanted, local_sem)
        to_scalar.start()
        to_scalar.wait()
        wait_bytes(mass_landed.at[pl.ds(0, half - 1)], recv_sem.at[MASS])

        def sums_of(row, whose):
            def add(i, sums):
                sums = list(sums)
                for j in range(per):
                    mass = mass_landed[i, row * per + j : row * per + j + 1, :]
                    w = wanted[i, 0, whose * per + j]
                    for k in range(cols):
                        sums[k] = sums[k] + mass * (w == k).astype(F32)
                return tuple(sums)

            return lax.fori_loop(0, half, add, tuple(jnp.zeros((1, blk), F32) for _ in range(cols)))

        mass_out[...] = jnp.zeros_like(mass_out)
        for k, mass in enumerate(sums_of(1, 1 - side)):
            mass_out[k : k + 1, :] = mass
        remote(mass_out, mass_far, MASS_DENSE, partner).start()
        for k, mass in enumerate(sums_of(0, side)):
            inverse[k : k + 1, :] = mass

    def efficiencies():
        wait_bytes(mass_far, recv_sem.at[MASS_DENSE])
        inverse[0:cols, :] = 1.0 / (inverse[0:cols, :] + mass_far[0:cols, :])

    def finish(c):
        sums = gather(c, 1)
        for k in range(cols):
            out[c * rc : (c + 1) * rc, k * blk : (k + 1) * blk] = (
                estimate[c, k] * sums[k] * inverse[k : k + 1, :]
            )

    chunks = range(chunk_count)
    for c in chunks:
        for b in range(rows):
            store_ratio(c, b, first_fold[b : b + 1])
        backward(c, 0, ((RELAY, other, relay_in),))
    for c in chunks:
        backward(c, 0, ((NEAR, base, near_in),))
    masses()
    for c in chunks:
        relay(c, 0)
    efficiencies()
    for c in chunks:
        update(c)
    for c in chunks:
        relay_pick(c)
    for c in chunks:
        fold(c)
        wait_sent(c, (PICK, RELAY_PICK))
        backward(c, 1, ((RELAY, other, relay_in),))
    for c in chunks:
        relay(c, 1)
        backward(c, 1, ((NEAR, base, near_in),))
    for c in chunks:
        finish(c)

    for c in chunks:
        wait_sent(c, (3 + RELAY, 3 + NEAR))
        wait_bytes(dense_out.at[c], send_sem.at[sem_of(c, 3 + DENSE)])
        wait_bytes(estimate.at[c], send_sem.at[sem_of(c, AHEAD)])
    wait_bytes(priors.at[pl.ds(0, n - 1)], send_sem.at[PRIOR])
    wait_bytes(wanted_landed.at[pl.ds(0, half - 1)], send_sem.at[WANTED])
    wait_bytes(mass_landed.at[pl.ds(0, half - 1)], send_sem.at[MASS])
    wait_bytes(mass_out, send_sem.at[MASS_DENSE])


def local(response, block_row, block_col, counts, prior):
    n = lax.axis_size("rows")
    half = n // 2
    slots, blk, _ = response.shape
    per = slots // n
    reps = counts.shape[0]
    rows = counts.shape[1] // blk
    cols = prior.shape[0] // blk
    rc = reps // CHUNKS
    tall = -(-cols // 8) * 8
    mass_rows = -(-2 * per // 8) * 8
    vmem = pl.BlockSpec(memory_space=pltpu.VMEM)
    hbm = pl.BlockSpec(memory_space=pl.ANY)
    smem = pl.BlockSpec(memory_space=pltpu.SMEM)
    sems = KINDS * CHUNKS + 4
    return pl.pallas_call(
        functools.partial(kernel, n, per, cols, rows, CHUNKS),
        out_shape=jax.ShapeDtypeStruct((reps, cols * blk), F32),
        in_specs=[hbm, smem, smem, hbm, vmem],
        out_specs=vmem,
        scratch_shapes=[
            pltpu.VMEM(counts.shape, counts.dtype),
            pltpu.VMEM((slots, blk, blk), F32),
            pltpu.VMEM((slots, 2 * blk, blk), BF16),
            pltpu.VMEM((half, 1, blk), jnp.int32),
            pltpu.VMEM((tall, blk), F32),
            pltpu.VMEM((n, tall, blk), F32),
            pltpu.VMEM((half, mass_rows, blk), F32),
            pltpu.VMEM((half, mass_rows, blk), F32),
            pltpu.VMEM((tall, blk), F32),
            pltpu.VMEM((tall, blk), F32),
            pltpu.VMEM((half, 1, blk), jnp.int32),
            pltpu.SMEM((half, 1, blk), jnp.int32),
            pltpu.VMEM((CHUNKS, slots, rc, blk), F32),
            pltpu.VMEM((CHUNKS, half * per, rc, blk), F32),
            pltpu.VMEM((CHUNKS, half * per, rc, blk), F32),
            pltpu.VMEM((CHUNKS, cols, rc, blk), F32),
            pltpu.VMEM((CHUNKS, cols, rc, blk), F32),
            pltpu.VMEM((CHUNKS, cols, rc, blk), F32),
            pltpu.VMEM((CHUNKS, cols, rc, blk), F32),
            pltpu.VMEM((CHUNKS, slots, rc, blk), F32),
            pltpu.VMEM((CHUNKS, cols, rc, blk), F32),
            pltpu.VMEM((rows * CHUNKS, 2 * rc, blk), BF16),
            pltpu.VMEM((tall, blk), F32),
            pltpu.SemaphoreType.DMA((sems,)),
            pltpu.SemaphoreType.DMA((sems,)),
            pltpu.SemaphoreType.DMA,
            pltpu.SemaphoreType.DMA((3,)),
        ],
        compiler_params=pltpu.CompilerParams(
            collective_id=0, has_side_effects=True, vmem_limit_bytes=60 * 1024 * 1024
        ),
    )(response, block_row, block_col, counts, prior.reshape(cols, blk))


def solution(mesh):
    in_specs = (
        P(("groups", "rows"), None, None),
        P(("groups", "rows")),
        P(("groups", "rows")),
        P(None, ("groups", "rows")),
        P(("groups", "rows")),
    )
    out_specs = P(None, ("groups", "rows"))
    return jax.shard_map(local, mesh=mesh, in_specs=in_specs, out_specs=out_specs, check_vma=False)
```
